32 devices in a mesh: row: 8 (over y, x, core), col: 4 (over z).
Axes of the slice: x: 2, y: 2, z: 4, core: 2. Of those that a mesh axis runs over, the one named last changes fastest.
Arguments:
- stiffness: bfloat16 [192, 27, 128, 128], P('row'), may hold values from -1.5 to 5, as said below
- block_cols: int32 [192, 27], P('row'), may hold values from 0 to 95, as said below
- block_row_counts: int32 [8], replicated, may hold values from 1 to 24, as said below
- start_basis: float32 [512, 24576], P('col', 'row'), may hold values from -6 to 6
Outputs:
- ritz_basis: float32 [512, 24576], P('col', 'row')
- projected: float32 [512, 512], P('col')
The draws below stay inside these ranges and needn't reach their ends.
Inputs may be any that keep to these rules, and one draw needn't show every extreme that they name: `block_cols`: on live slots the 27 entries name the global block rows coupled to that slot's block row, its own among them; dead slots hold entries of the same kind. `block_row_counts`: the counts sum to 96, and one index holds exactly 24. Over live slots the stiffness is symmetric: the blocks that couple global block rows g and h are the transposes of those that couple h and g.
All inputs are finite; a program needn't handle non-finite values.
Results may differ from the reference program's by a relative error of at most 0.013.
Values may be sent and summed in bfloat16 or wider, within the bound.
A program may use at most 128 MiB of HBM per device.

```python
import math
import jax
import jax.numpy as jnp
from jax import lax

B = 128
M = 512
CAP = 24
NB = 96
PSLOTS = 192
NDOF = 12288


neighbour_steps = [(shift_x, shift_y, shift_z) for shift_x in (-1, 0, 1) for shift_y in (-1, 0, 1) for shift_z in (-1, 0, 1)]


upward_steps = [offset for offset in neighbour_steps if offset > (0, 0, 0)]


def layout(key):
    row_devices = PSLOTS // CAP
    heavy_index = jax.random.randint(jax.random.fold_in(key, 101), (), 0, row_devices)
    spare_slots = (row_devices - 1) * (CAP - 1)
    extra_units = NB - CAP - (row_devices - 1)
    shuffled = jax.random.permutation(jax.random.fold_in(key, 202), spare_slots)
    chosen = shuffled[:extra_units] // (CAP - 1)
    others = 1 + jnp.sum((chosen[:, None] == jnp.arange(row_devices - 1)[None, :]).astype(jnp.int32), 0)
    device_index = jnp.arange(row_devices)
    source = jnp.clip(jnp.where(device_index < heavy_index, device_index, device_index - 1), 0, row_devices - 2)
    row_counts = jnp.where(device_index == heavy_index, CAP, others[source]).astype(jnp.int32)
    block_ends = jnp.cumsum(row_counts).astype(jnp.int32)
    block_starts = block_ends - row_counts
    slot_index = jnp.arange(PSLOTS)
    global_row = ((block_starts[slot_index // CAP] + slot_index % CAP) % NB).astype(jnp.int32)
    return (row_counts, global_row)


def moved(slot_cell, offset):
    grid_depth = NB // 16
    along_x = slot_cell // (8 * grid_depth)
    along_y = slot_cell // grid_depth % 8
    along_z = slot_cell % grid_depth
    return (along_x + offset[0]) % 2 * 8 * grid_depth + (along_y + offset[1]) % 8 * grid_depth + (along_z + offset[2]) % grid_depth


def draw_block_row_counts(key, part):
    return layout(key)[0]


def draw_block_cols(key, part):
    row_counts, global_row = layout(key)
    return jnp.stack([moved(global_row, offset) for offset in neighbour_steps], 1).astype(jnp.int32)


def draw_stiffness(key, part):
    row_counts, global_row = layout(key)
    slot_cell = global_row
    entry_scale = 1.0 / math.sqrt(27.0 * B)
    pair_blocks = jax.random.normal(jax.random.fold_in(key, 404), (NB, 13, B, B), jnp.float32) * entry_scale
    self_blocks = jax.random.normal(jax.random.fold_in(key, 505), (NB, B, B), jnp.float32) * entry_scale
    diagonal_values = jax.random.uniform(jax.random.fold_in(key, 606), (NB, B), jnp.float32, 2.0, 4.0)
    identity = jnp.eye(B, dtype=jnp.float32)
    stacked = []
    for offset in neighbour_steps:
        if offset == (0, 0, 0):
            own_block = self_blocks[slot_cell]
            stacked.append((own_block + jnp.swapaxes(own_block, 1, 2)) * 0.70710678 + diagonal_values[slot_cell][:, :, None] * identity[None, :, :])
        elif offset in upward_steps:
            stacked.append(pair_blocks[slot_cell, upward_steps.index(offset)])
        else:
            mirror = (-offset[0], -offset[1], -offset[2])
            stacked.append(jnp.swapaxes(pair_blocks[moved(slot_cell, offset), upward_steps.index(mirror)], 1, 2))
    return jnp.stack(stacked, 1).astype(jnp.bfloat16)


def block_scale(own_key, dims, shards, least, high):
    def one(position, parts):
        steps = jax.random.uniform(jax.random.fold_in(jax.random.fold_in(own_key, 6), position), (parts,), jnp.float32, least / len(shards), high / len(shards))
        return jnp.repeat(jnp.exp(steps), dims[position] // parts).reshape((-1,) + (1,) * (len(dims) - position - 1))

    level = one(*shards[0])
    for cut in shards[1:]:
        level = level * one(*cut)
    return level


def scatter_about(own_key, shape, scale, reach, pieces=(), held_as=jnp.bfloat16):
    drawn = jax.random.normal(own_key, shape, jnp.float32) * scale
    if len(pieces) > 0:
        drawn = block_scale(own_key, shape, pieces, -0.22, 0.18) * drawn
    return jnp.clip(drawn, min=-reach, max=reach).astype(held_as)


def setup_inputs(seed: int = 0) -> dict:
    key_list = jax.random.split(jax.random.key(seed), 5)
    return {
        "stiffness": draw_stiffness(jax.random.fold_in(key_list[4], 71), 0),
        "block_cols": draw_block_cols(jax.random.fold_in(key_list[4], 71), 0),
        "block_row_counts": draw_block_row_counts(jax.random.fold_in(key_list[4], 71), 0),
        "start_basis": scatter_about(key_list[3], (M, PSLOTS * B), 1.0, 6.0, ((0, 4), (1, 8)), jnp.float32),
    }


center_value = 4.0
half_width = 1.5
ridge_shift = 0.5

def slot_positions(columns, row_counts):
    block_ends = jnp.cumsum(row_counts).astype(jnp.int32)
    block_starts = (block_ends - row_counts).astype(jnp.int32)
    owner_index = jnp.sum((block_ends[None, None, :] <= columns[:, :, None]).astype(jnp.int32), 2).astype(jnp.int32)
    device_ids = jnp.arange(row_counts.shape[0], dtype=jnp.int32)
    first_block = jnp.sum(jnp.where(owner_index[:, :, None] == device_ids[None, None, :], block_starts[None, None, :], 0), 2).astype(jnp.int32)
    return (owner_index * CAP + columns - first_block).astype(jnp.int32)

def reference(stiffness, block_cols, block_row_counts, start_basis):
    slot_index = jnp.arange(PSLOTS, dtype=jnp.int32)
    live_slots = jnp.where(slot_index % CAP < block_row_counts[slot_index // CAP], 1.0, 0.0).astype(jnp.float32)
    live_columns = jnp.repeat(live_slots, B)
    positions = slot_positions(block_cols, block_row_counts)

    def apply_stiffness(panel):
        blocks = panel.reshape(M, PSLOTS, B)

        def one_slot(slot):
            picked = jnp.take(blocks, positions[slot], axis=1).astype(jnp.float32)
            return jnp.einsum('mkb,kab->ma', picked, stiffness[slot].astype(jnp.float32), precision=lax.Precision.HIGHEST)
        result = lax.map(one_slot, slot_index)
        result = result * live_slots[:, None, None]
        return jnp.transpose(result, (1, 0, 2)).reshape(M, PSLOTS * B)
    start_field = start_basis * live_columns[None, :]
    degree_one = (apply_stiffness(start_field.astype(jnp.bfloat16)) - center_value * start_field) / half_width
    degree_two = 2.0 * (apply_stiffness(degree_one.astype(jnp.bfloat16)) - center_value * degree_one) / half_width - start_field
    degree_three = 2.0 * (apply_stiffness(degree_two.astype(jnp.bfloat16)) - center_value * degree_two) / half_width - degree_one
    identity = jnp.eye(M, dtype=jnp.float32)
    gram_matrix = jnp.dot(degree_three.astype(jnp.float32), degree_three.T.astype(jnp.float32), precision=lax.Precision.HIGHEST, preferred_element_type=jnp.float32) / NDOF + ridge_shift * identity
    lower_factor = jnp.linalg.cholesky(gram_matrix)
    ritz_basis = lax.linalg.triangular_solve(lower_factor, degree_three, left_side=True, lower=True)
    stiff_image = apply_stiffness(ritz_basis.astype(jnp.bfloat16))
    projected = jnp.dot(stiff_image.astype(jnp.float32), ritz_basis.T.astype(jnp.float32), precision=lax.Precision.HIGHEST, preferred_element_type=jnp.float32) / NDOF
    return (ritz_basis, projected)
```

```python
import functools

import jax
import jax.numpy as jnp
from jax import lax
from jax.experimental import pallas as pl
from jax.experimental.pallas import tpu as pltpu
from jax.sharding import PartitionSpec as P

center_value = 4.0
half_width = 1.5
ridge_shift = 0.5

MESH = pl.DeviceIdType.MESH
HIGH = lax.Precision.HIGHEST
NT = (((1,), (1,)), ((), ()))
NN = (((1,), (0,)), ((), ()))


def gather_kernel(slots, own_ref, out_ref, send_sems, recv_sems, local_sem):
    me = lax.axis_index("row")
    half = slots // 2
    core = me % 2
    along_x = (me // 2) % 2
    along_y = me // 4
    mate = me + 1 - 2 * core
    beside = me + 2 - 4 * along_x
    above = me + 4 - 8 * along_y
    across = beside + 4 - 8 * along_y

    barrier = pltpu.get_barrier_semaphore()
    for other in (mate, beside, above):
        pl.semaphore_signal(barrier, inc=1, device_id={"row": other}, device_id_type=MESH)
    pl.semaphore_wait(barrier, 3)

    def place(device, part):
        return out_ref.at[pl.ds(device * slots + part * half, half)]

    def own(part):
        return own_ref.at[pl.ds(part * half, half)]

    def send(number, source, device, part, target):
        return pltpu.make_async_remote_copy(
            src_ref=source,
            dst_ref=place(device, part),
            send_sem=send_sems.at[number],
            recv_sem=recv_sems.at[number],
            device_id={"row": target},
            device_id_type=MESH,
        )

    copies = [
        send(0, own(0), me, 0, beside),
        send(1, own(1), me, 1, beside),
        send(2, own(0), me, 0, above),
        send(3, own(1), me, 1, above),
        send(4, place(beside, 0), beside, 0, above),
        send(5, place(above, 1), above, 1, beside),
        send(6, own(0), me, 0, mate),
        send(7, own(1), me, 1, mate),
        send(8, place(beside, 0), beside, 0, mate),
        send(9, place(beside, 1), beside, 1, mate),
        send(10, place(above, 0), above, 0, mate),
        send(11, place(above, 1), above, 1, mate),
        send(12, place(across, 0), across, 0, mate),
        send(13, place(across, 1), across, 1, mate),
    ]
    for number in (0, 3, 1, 2, 6, 7):
        copies[number].start()
    keep = pltpu.make_async_copy(own_ref, out_ref.at[pl.ds(me * slots, slots)], local_sem)
    keep.start()
    for arrived, onward in ((0, (4, 8)), (3, (5, 11)), (1, (9,)), (2, (10,)), (4, (12,)), (5, (13,))):
        copies[arrived].wait_recv()
        for number in onward:
            copies[number].start()
    for number in range(6, 14):
        copies[number].wait_recv()
    keep.wait()
    for copy in copies:
        copy.wait_send()


def gather_rows(panel):
    slots, modes, size = panel.shape
    rows = lax.axis_size("row")
    if rows != 8:
        return lax.all_gather(panel, "row", axis=0, tiled=True)
    return pl.pallas_call(
        functools.partial(gather_kernel, slots),
        out_shape=jax.ShapeDtypeStruct((rows * slots, modes, size), panel.dtype),
        in_specs=[pl.BlockSpec(memory_space=pl.ANY)],
        out_specs=pl.BlockSpec(memory_space=pl.ANY),
        scratch_shapes=[
            pltpu.SemaphoreType.DMA((14,)),
            pltpu.SemaphoreType.DMA((14,)),
            pltpu.SemaphoreType.DMA,
        ],
        compiler_params=pltpu.CompilerParams(collective_id=0, has_side_effects=True),
        name="gather_rows",
    )(panel)


def product(positions, blocks_ref, stiff_ref):
    slot = pl.program_id(0)
    neighbours = stiff_ref.shape[1]
    picked = jnp.concatenate([blocks_ref[positions[slot, k]] for k in range(neighbours)], axis=1)
    stored = jnp.concatenate([stiff_ref[0, k] for k in range(neighbours)], axis=1)
    return lax.dot_general(picked, stored, NT, preferred_element_type=jnp.float32)


def step_kernel(scale, positions, own_count, blocks_ref, stiff_ref, now_ref, before_ref, out_ref, copy_ref):
    live = pl.program_id(0) < own_count[0]

    @pl.when(live)
    def _():
        now = now_ref[0]
        result = (product(positions, blocks_ref, stiff_ref) - center_value * now) * (scale / half_width)
        if scale == 2.0:
            result = result - before_ref[0]
        out_ref[0] = result
        copy_ref[0] = result.astype(copy_ref.dtype)

    @pl.when(jnp.logical_not(live))
    def _():
        out_ref[...] = jnp.zeros_like(out_ref)
        copy_ref[...] = jnp.zeros_like(copy_ref)


def last_kernel(positions, own_count, blocks_ref, stiff_ref, now_ref, all_ref, out_ref):
    slot = pl.program_id(0)

    @pl.when(slot == 0)
    def _():
        out_ref[...] = jnp.zeros_like(out_ref)

    @pl.when(slot < own_count[0])
    def _():
        image = product(positions, blocks_ref, stiff_ref).astype(jnp.bfloat16)
        left = jnp.concatenate([now_ref[0], image], axis=0)
        whole = all_ref[...].reshape(-1, all_ref.shape[-1])
        out_ref[...] += lax.dot_general(left, whole, NT, preferred_element_type=jnp.float32)


def apply_call(kernel, positions, own_count, blocks, stiffness, extra, extra_specs, out_shape, out_specs):
    slots, neighbours, size, _ = stiffness.shape
    last = lambda slot, pos, count: (jnp.minimum(slot, count[0] - 1), 0, 0, 0)
    return pl.pallas_call(
        kernel,
        grid_spec=pltpu.PrefetchScalarGridSpec(
            num_scalar_prefetch=2,
            grid=(slots,),
            in_specs=[
                pl.BlockSpec(memory_space=pltpu.VMEM),
                pl.BlockSpec((1, neighbours, size, size), last),
                *extra_specs,
            ],
            out_specs=out_specs,
        ),
        out_shape=out_shape,
        compiler_params=pltpu.CompilerParams(vmem_limit_bytes=40 * 2**20),
    )(positions, own_count, blocks, stiffness, *extra)


def eliminate(block_ref, work_ref):
    size = block_ref.shape[0]
    rows = lax.broadcasted_iota(jnp.int32, (size, size), 0)
    columns = lax.broadcasted_iota(jnp.int32, (size, size), 1)
    work_ref[...] = (rows == columns).astype(jnp.float32)
    down = lax.broadcasted_iota(jnp.int32, (size, 1), 0)
    across = lax.broadcasted_iota(jnp.int32, (1, size), 1)

    def step(k, carry):
        pivot_row = block_ref[pl.ds(k, 1), :]
        work_row = work_ref[pl.ds(k, 1), :]
        pivot = jnp.sum(jnp.where(across == k, pivot_row, 0.0), axis=1, keepdims=True)
        root = lax.rsqrt(pivot)
        block = block_ref[...]
        column = jnp.sum(jnp.where(columns == k, block, 0.0), axis=1, keepdims=True)
        factor = jnp.where(down > k, column * (root * root), 0.0)
        block_ref[...] = block - factor * pivot_row
        work_ref[...] = jnp.where(down == k, work_ref[...] * root, work_ref[...] - factor * work_row)
        return carry

    lax.fori_loop(0, size, step, 0)


def dot(a, b, dims=NN):
    return lax.dot_general(a, b, dims, precision=HIGH, preferred_element_type=jnp.float32)


def factor_kernel(gram_ref, inverse_ref, trail, block_ref, work_ref):
    modes = gram_ref.shape[0]
    size = block_ref.shape[0]
    trail[...] = gram_ref[...]
    inverse_ref[...] = jnp.zeros_like(inverse_ref)
    for start in range(0, modes, size):
        end = start + size
        block_ref[...] = trail[start:end, start:end]
        eliminate(block_ref, work_ref)
        own = work_ref[...]
        inverse_ref[start:end, start:end] = own
        if start:
            left = dot(trail[start:end, :start], inverse_ref[:start, :start])
            inverse_ref[start:end, :start] = -dot(own, left)
        if end < modes:
            panel = dot(trail[end:, start:end], own, NT)
            trail[end:, start:end] = panel
            trail[end:, end:] = trail[end:, end:] - dot(panel, panel, NT)


def factor_inverse(gram):
    modes = gram.shape[0]
    return pl.pallas_call(
        factor_kernel,
        out_shape=jax.ShapeDtypeStruct((modes, modes), jnp.float32),
        in_specs=[pl.BlockSpec(memory_space=pltpu.VMEM)],
        out_specs=pl.BlockSpec(memory_space=pltpu.VMEM),
        scratch_shapes=[
            pltpu.VMEM((modes, modes), jnp.float32),
            pltpu.VMEM((128, 128), jnp.float32),
            pltpu.VMEM((128, 128), jnp.float32),
        ],
        compiler_params=pltpu.CompilerParams(vmem_limit_bytes=32 * 2**20),
        name="factor_inverse",
    )(gram)


def ritz_kernel(rows_ref, all_ref, out_ref):
    whole = all_ref[...].reshape(-1, all_ref.shape[-1])
    out_ref[...] = lax.dot_general(rows_ref[...], whole, NN, preferred_element_type=jnp.float32)


def local(stiffness, block_cols, block_row_counts, start_basis):
    slots, neighbours, size, _ = stiffness.shape
    modes = start_basis.shape[0]
    groups = lax.axis_size("col")
    rows = block_row_counts.shape[0]
    row_position = lax.axis_index("row")
    ids = jnp.arange(rows, dtype=jnp.int32)
    starts = jnp.sum(jnp.where(ids[None, :] < ids[:, None], block_row_counts[None, :], 0), 1)
    ends = starts + block_row_counts
    own_count = jnp.sum(jnp.where(ids == row_position, block_row_counts, 0))
    passed = (ends[None, None, :] <= block_cols[:, :, None]).astype(jnp.int32)
    owner = jnp.sum(passed, 2)
    first = jnp.sum(passed * block_row_counts[None, None, :], 2)
    positions = (owner * slots + block_cols - first).astype(jnp.int32)
    total = (jnp.sum(block_row_counts) * size).astype(jnp.float32)
    live = (jnp.arange(slots) < own_count).astype(jnp.float32)
    own_count = own_count.reshape(1)

    block = lambda: pl.BlockSpec((1, modes, size), lambda slot, pos, count: (slot, 0, 0))
    shape = (slots, modes, size)

    def advance(scale, now, now_copy, before):
        return apply_call(
            functools.partial(step_kernel, scale),
            positions,
            own_count,
            gather_rows(now_copy),
            stiffness,
            (now, before),
            [block(), block()],
            (jax.ShapeDtypeStruct(shape, jnp.float32), jax.ShapeDtypeStruct(shape, jnp.bfloat16)),
            (block(), block()),
        )

    x0 = jnp.swapaxes(start_basis.reshape(modes, slots, size), 0, 1) * live[:, None, None]
    y1, y1_copy = advance(1.0, x0, x0.astype(jnp.bfloat16), x0)
    y2, y2_copy = advance(2.0, y1, y1_copy, x0)
    y3, y3_copy = advance(2.0, y2, y2_copy, y1)

    every = lax.all_gather(y3_copy, "col", axis=0, tiled=False)
    all_modes = groups * modes
    all_block = lambda: pl.BlockSpec(
        (groups, 1, modes, size), lambda slot, *unused: (0, slot, 0, 0)
    )
    sums = apply_call(
        last_kernel,
        positions,
        own_count,
        gather_rows(y3_copy),
        stiffness,
        (y3_copy, every),
        [block(), all_block()],
        jax.ShapeDtypeStruct((2 * modes, all_modes), jnp.float32),
        pl.BlockSpec((2 * modes, all_modes), lambda slot, *unused: (0, 0)),
    )
    part = lax.psum_scatter(sums.reshape(2, rows, modes // rows, all_modes), "row", scatter_dimension=1, tiled=True)
    gram = lax.all_gather(part[0, 0], ("col", "row"), axis=0, tiled=True)
    images = lax.all_gather(part[1, 0].astype(jnp.bfloat16), ("col", "row"), axis=0, tiled=True)
    gram = gram / total + ridge_shift * jnp.eye(all_modes, dtype=jnp.float32)
    inverse = factor_inverse(gram)
    own_inverse = lax.dynamic_slice_in_dim(inverse, lax.axis_index("col") * modes, modes, 0)
    ritz = pl.pallas_call(
        ritz_kernel,
        grid=(slots,),
        in_specs=[pl.BlockSpec((modes, all_modes), lambda slot: (0, 0)), all_block()],
        out_specs=pl.BlockSpec((modes, size), lambda slot: (0, slot)),
        out_shape=jax.ShapeDtypeStruct((modes, slots * size), jnp.float32),
    )(own_inverse.astype(jnp.bfloat16), every)
    turned = dot(own_inverse, images.astype(jnp.float32))
    projected = dot(turned, inverse, NT) / total
    return (ritz, projected)


def solution(mesh):
    in_specs = (P("row", None, None, None), P("row", None), P(), P("col", "row"))
    out_specs = (P("col", "row"), P("col", None))
    return jax.shard_map(local, mesh=mesh, in_specs=in_specs, out_specs=out_specs, check_vma=False)
```

```python
import functools

import jax
import jax.numpy as jnp
from jax import lax
from jax.experimental import pallas as pl
from jax.experimental.pallas import tpu as pltpu
from jax.sharding import PartitionSpec as P

center_value = 4.0
half_width = 1.5
ridge_shift = 0.5

MESH = pl.DeviceIdType.MESH
HIGH = lax.Precision.HIGHEST
NT = (((1,), (1,)), ((), ()))
NN = (((1,), (0,)), ((), ()))


def line_copy(panel_ref, every_ref, sems, step, side):
    me = lax.axis_index("col")
    groups = every_ref.shape[0]
    target = me + side
    source = me - side * step
    sends = (target >= 0) & (target < groups) & (source >= 0) & (source < groups)
    origin = source - side
    receives = (origin >= 0) & (origin < groups)
    number = 2 * step + (1 if side > 0 else 0)
    bounded = lax.rem(source + groups, groups)
    return sends, receives, pltpu.make_async_remote_copy(
        src_ref=panel_ref if step == 0 else every_ref.at[bounded],
        dst_ref=every_ref.at[bounded],
        send_sem=sems.at[0, number],
        recv_sem=sems.at[1, number],
        device_id={"col": lax.rem(target + groups, groups)},
        device_id_type=MESH,
    )


def gather_kernel(slots, line, own_ref, out_ref, *refs):
    if line:
        every_ref, send_sems, recv_sems, local_sem, line_sems = refs
    else:
        send_sems, recv_sems, local_sem = refs
    me = lax.axis_index("row")
    half = slots // 2
    core = me % 2
    along_x = (me // 2) % 2
    along_y = me // 4
    mate = me + 1 - 2 * core
    beside = me + 2 - 4 * along_x
    above = me + 4 - 8 * along_y
    across = beside + 4 - 8 * along_y

    barrier = pltpu.get_barrier_semaphore()
    for other in (mate, beside, above):
        pl.semaphore_signal(barrier, inc=1, device_id={"row": other}, device_id_type=MESH)
    if line:
        groups = every_ref.shape[0]
        level = lax.axis_index("col")

        @pl.when(level > 0)
        def _():
            pl.semaphore_signal(barrier, inc=1, device_id={"col": level - 1}, device_id_type=MESH)

        @pl.when(level < groups - 1)
        def _():
            pl.semaphore_signal(barrier, inc=1, device_id={"col": level + 1}, device_id_type=MESH)

        neighbours = (level > 0).astype(jnp.int32) + (level < groups - 1).astype(jnp.int32)
        pl.semaphore_wait(barrier, 3 + neighbours)
    else:
        pl.semaphore_wait(barrier, 3)

    def line_start(step):
        for side in (-1, 1):
            sends, _, copy = line_copy(own_ref, every_ref, line_sems, step, side)
            pl.when(sends)(copy.start)

    def line_wait(step):
        for side in (-1, 1):
            _, receives, copy = line_copy(own_ref, every_ref, line_sems, step, side)
            pl.when(receives & (level - side >= 0) & (level - side < groups))(copy.wait_recv)

    def line_end(step):
        for side in (-1, 1):
            sends, _, copy = line_copy(own_ref, every_ref, line_sems, step, side)
            pl.when(sends)(copy.wait_send)

    def place(device, part):
        return out_ref.at[pl.ds(device * slots + part * half, half)]

    def own(part):
        return own_ref.at[pl.ds(part * half, half)]

    def send(number, source, device, part, target):
        return pltpu.make_async_remote_copy(
            src_ref=source,
            dst_ref=place(device, part),
            send_sem=send_sems.at[number],
            recv_sem=recv_sems.at[number],
            device_id={"row": target},
            device_id_type=MESH,
        )

    copies = [
        send(0, own(0), me, 0, beside),
        send(1, own(1), me, 1, beside),
        send(2, own(0), me, 0, above),
        send(3, own(1), me, 1, above),
        send(4, place(beside, 0), beside, 0, above),
        send(5, place(above, 1), above, 1, beside),
        send(6, own(0), me, 0, mate),
        send(7, own(1), me, 1, mate),
        send(8, place(beside, 0), beside, 0, mate),
        send(9, place(beside, 1), beside, 1, mate),
        send(10, place(above, 0), above, 0, mate),
        send(11, place(above, 1), above, 1, mate),
        send(12, place(across, 0), across, 0, mate),
        send(13, place(across, 1), across, 1, mate),
    ]
    for number in (0, 3, 1, 2, 6, 7):
        copies[number].start()
    keep = [pltpu.make_async_copy(own_ref, out_ref.at[pl.ds(me * slots, slots)], local_sem.at[0])]
    if line:
        line_start(0)
        keep.append(pltpu.make_async_copy(own_ref, every_ref.at[level], local_sem.at[1]))
    for copy in keep:
        copy.start()
    for arrived, onward in ((0, (4, 8)), (3, (5, 11)), (1, (9,)), (2, (10,))):
        copies[arrived].wait_recv()
        for number in onward:
            copies[number].start()
    if line:
        line_wait(0)
        line_start(1)
    for arrived, onward in ((4, 12), (5, 13)):
        copies[arrived].wait_recv()
        copies[onward].start()
    for number in range(6, 14):
        copies[number].wait_recv()
    if line:
        for step in range(1, groups - 1):
            line_wait(step)
            if step < groups - 2:
                line_start(step + 1)
        for step in range(groups - 1):
            line_end(step)
    for copy in keep:
        copy.wait()
    for copy in copies:
        copy.wait_send()


def gather_rows(panel, number, line=False):
    slots, modes, size = panel.shape
    rows, groups = lax.axis_size("row"), lax.axis_size("col")
    if rows != 8 or groups < 3:
        out = lax.all_gather(panel, "row", axis=0, tiled=True)
        return (out, lax.all_gather(panel, "col", axis=0, tiled=False)) if line else out
    out_shape = [jax.ShapeDtypeStruct((rows * slots, modes, size), panel.dtype)]
    scratch = [
        pltpu.SemaphoreType.DMA((14,)),
        pltpu.SemaphoreType.DMA((14,)),
        pltpu.SemaphoreType.DMA((2,)),
    ]
    if line:
        out_shape.append(jax.ShapeDtypeStruct((groups, slots, modes, size), panel.dtype))
        scratch.append(pltpu.SemaphoreType.DMA((2, 2 * (groups - 1))))
    out = pl.pallas_call(
        functools.partial(gather_kernel, slots, line),
        out_shape=out_shape,
        in_specs=[pl.BlockSpec(memory_space=pl.ANY)],
        out_specs=[pl.BlockSpec(memory_space=pl.ANY)] * len(out_shape),
        scratch_shapes=scratch,
        compiler_params=pltpu.CompilerParams(collective_id=number, has_side_effects=True),
        name="gather_both" if line else "gather_rows",
    )(panel)
    return out if line else out[0]


def reduce_kernel(sums_ref, out_ref, landed, total, row_sems, col_sems):
    rows, groups = landed.shape[0], total.shape[0]
    me, level = lax.axis_index("row"), lax.axis_index("col")
    peers = [lax.rem(me + shift, rows) for shift in range(1, rows)]
    levels = [lax.rem(level + shift, groups) for shift in range(1, groups)]
    barrier = pltpu.get_barrier_semaphore()
    for peer in peers:
        pl.semaphore_signal(barrier, inc=1, device_id={"row": peer}, device_id_type=MESH)
    for other in levels:
        pl.semaphore_signal(barrier, inc=1, device_id={"col": other}, device_id_type=MESH)
    pl.semaphore_wait(barrier, rows + groups - 2)
    shares = []
    for number, peer in enumerate(peers):
        copy = pltpu.make_async_remote_copy(
            src_ref=sums_ref.at[peer],
            dst_ref=landed.at[number],
            send_sem=row_sems.at[0, number],
            recv_sem=row_sems.at[1, number],
            device_id={"row": peer},
            device_id_type=MESH,
        )
        copy.start()
        shares.append(copy)
    share = sums_ref[me]
    for number, copy in enumerate(shares):
        copy.wait_recv()
        share = share + landed[number]
    total[0] = share
    out_ref[level] = share
    exchanges = []
    for number, other in enumerate(levels):
        copy = pltpu.make_async_remote_copy(
            src_ref=total.at[0],
            dst_ref=total.at[number + 1],
            send_sem=col_sems.at[0, number],
            recv_sem=col_sems.at[1, number],
            device_id={"col": other},
            device_id_type=MESH,
        )
        copy.start()
        exchanges.append(copy)
    for number, copy in enumerate(exchanges):
        copy.wait_recv()
        out_ref[lax.rem(level + groups - number - 1, groups)] = total[number + 1]
    for copy in shares + exchanges:
        copy.wait_send()


def reduce_sums(sums):
    rows, groups = lax.axis_size("row"), lax.axis_size("col")
    if rows != 8 or groups < 3:
        share = lax.psum_scatter(sums, "row", scatter_dimension=0, tiled=False)
        return lax.all_gather(share, "col", axis=0, tiled=False)
    return pl.pallas_call(
        reduce_kernel,
        out_shape=jax.ShapeDtypeStruct((groups, *sums.shape[1:]), sums.dtype),
        in_specs=[pl.BlockSpec(memory_space=pltpu.VMEM)],
        out_specs=pl.BlockSpec(memory_space=pltpu.VMEM),
        scratch_shapes=[
            pltpu.VMEM(sums.shape, sums.dtype),
            pltpu.VMEM((groups, *sums.shape[1:]), sums.dtype),
            pltpu.SemaphoreType.DMA((2, rows)),
            pltpu.SemaphoreType.DMA((2, groups)),
        ],
        compiler_params=pltpu.CompilerParams(collective_id=3, has_side_effects=True),
        name="reduce_sums",
    )(sums)


def product(positions, blocks_ref, stiff_ref):
    slot = pl.program_id(0)
    neighbours = stiff_ref.shape[1]
    picked = jnp.concatenate([blocks_ref[positions[slot, k]] for k in range(neighbours)], axis=1)
    stored = jnp.concatenate([stiff_ref[0, k] for k in range(neighbours)], axis=1)
    return lax.dot_general(picked, stored, NT, preferred_element_type=jnp.float32)


def step_kernel(scale, positions, own_count, blocks_ref, stiff_ref, now_ref, before_ref, out_ref, copy_ref):
    live = pl.program_id(0) < own_count[0]

    @pl.when(live)
    def _():
        now = now_ref[0]
        result = (product(positions, blocks_ref, stiff_ref) - center_value * now) * (scale / half_width)
        if scale == 2.0:
            result = result - before_ref[0]
        out_ref[0] = result
        copy_ref[0] = result.astype(copy_ref.dtype)

    @pl.when(jnp.logical_not(live))
    def _():
        out_ref[...] = jnp.zeros_like(out_ref)
        copy_ref[...] = jnp.zeros_like(copy_ref)


def last_kernel(positions, own_count, blocks_ref, stiff_ref, now_ref, all_ref, out_ref):
    slot = pl.program_id(0)

    @pl.when(slot == 0)
    def _():
        out_ref[...] = jnp.zeros_like(out_ref)

    @pl.when(slot < own_count[0])
    def _():
        image = product(positions, blocks_ref, stiff_ref).astype(jnp.bfloat16)
        left = jnp.concatenate([now_ref[0], image], axis=0)
        whole = all_ref[...].reshape(-1, all_ref.shape[-1])
        out_ref[...] += lax.dot_general(left, whole, NT, preferred_element_type=jnp.float32)


def apply_call(kernel, positions, own_count, blocks, stiffness, extra, extra_specs, out_shape, out_specs):
    slots, neighbours, size, _ = stiffness.shape
    last = lambda slot, pos, count: (jnp.minimum(slot, count[0] - 1), 0, 0, 0)
    return pl.pallas_call(
        kernel,
        grid_spec=pltpu.PrefetchScalarGridSpec(
            num_scalar_prefetch=2,
            grid=(slots,),
            in_specs=[
                pl.BlockSpec(memory_space=pltpu.VMEM),
                pl.BlockSpec((1, neighbours, size, size), last),
                *extra_specs,
            ],
            out_specs=out_specs,
        ),
        out_shape=out_shape,
        compiler_params=pltpu.CompilerParams(vmem_limit_bytes=40 * 2**20),
    )(positions, own_count, blocks, stiffness, *extra)


def eliminate(block_ref, work_ref):
    size = block_ref.shape[0]
    rows = lax.broadcasted_iota(jnp.int32, (size, size), 0)
    columns = lax.broadcasted_iota(jnp.int32, (size, size), 1)
    work_ref[...] = (rows == columns).astype(jnp.float32)
    down = lax.broadcasted_iota(jnp.int32, (size, 1), 0)
    across = lax.broadcasted_iota(jnp.int32, (1, size), 1)

    def step(k, carry):
        pivot_row = block_ref[pl.ds(k, 1), :]
        work_row = work_ref[pl.ds(k, 1), :]
        pivot = jnp.sum(jnp.where(across == k, pivot_row, 0.0), axis=1, keepdims=True)
        root = lax.rsqrt(pivot)
        block = block_ref[...]
        column = jnp.sum(jnp.where(columns == k, block, 0.0), axis=1, keepdims=True)
        factor = jnp.where(down > k, column * (root * root), 0.0)
        block_ref[...] = block - factor * pivot_row
        work_ref[...] = jnp.where(down == k, work_ref[...] * root, work_ref[...] - factor * work_row)
        return carry

    lax.fori_loop(0, size, step, 0)


def dot(a, b, dims=NN):
    return lax.dot_general(a, b, dims, precision=HIGH, preferred_element_type=jnp.float32)


def factor_kernel(gram_ref, inverse_ref, trail, block_ref, work_ref):
    modes = gram_ref.shape[0]
    size = block_ref.shape[0]
    trail[...] = gram_ref[...]
    inverse_ref[...] = jnp.zeros_like(inverse_ref)
    for start in range(0, modes, size):
        end = start + size
        block_ref[...] = trail[start:end, start:end]
        eliminate(block_ref, work_ref)
        own = work_ref[...]
        inverse_ref[start:end, start:end] = own
        if start:
            left = dot(trail[start:end, :start], inverse_ref[:start, :start])
            inverse_ref[start:end, :start] = -dot(own, left)
        if end < modes:
            panel = dot(trail[end:, start:end], own, NT)
            trail[end:, start:end] = panel
            trail[end:, end:] = trail[end:, end:] - dot(panel, panel, NT)


def factor_inverse(gram):
    modes = gram.shape[0]
    return pl.pallas_call(
        factor_kernel,
        out_shape=jax.ShapeDtypeStruct((modes, modes), jnp.float32),
        in_specs=[pl.BlockSpec(memory_space=pltpu.VMEM)],
        out_specs=pl.BlockSpec(memory_space=pltpu.VMEM),
        scratch_shapes=[
            pltpu.VMEM((modes, modes), jnp.float32),
            pltpu.VMEM((128, 128), jnp.float32),
            pltpu.VMEM((128, 128), jnp.float32),
        ],
        compiler_params=pltpu.CompilerParams(vmem_limit_bytes=32 * 2**20),
        name="factor_inverse",
    )(gram)


def ritz_kernel(rows_ref, all_ref, out_ref):
    whole = all_ref[...].reshape(-1, all_ref.shape[-1])
    out_ref[...] = lax.dot_general(rows_ref[...], whole, NN, preferred_element_type=jnp.float32)


def local(stiffness, block_cols, block_row_counts, start_basis):
    slots, neighbours, size, _ = stiffness.shape
    modes = start_basis.shape[0]
    groups = lax.axis_size("col")
    rows = block_row_counts.shape[0]
    row_position = lax.axis_index("row")
    ids = jnp.arange(rows, dtype=jnp.int32)
    starts = jnp.sum(jnp.where(ids[None, :] < ids[:, None], block_row_counts[None, :], 0), 1)
    ends = starts + block_row_counts
    own_count = jnp.sum(jnp.where(ids == row_position, block_row_counts, 0))
    passed = (ends[None, None, :] <= block_cols[:, :, None]).astype(jnp.int32)
    owner = jnp.sum(passed, 2)
    first = jnp.sum(passed * block_row_counts[None, None, :], 2)
    positions = (owner * slots + block_cols - first).astype(jnp.int32)
    total = (jnp.sum(block_row_counts) * size).astype(jnp.float32)
    live = (jnp.arange(slots) < own_count).astype(jnp.float32)
    own_count = own_count.reshape(1)

    block = lambda: pl.BlockSpec((1, modes, size), lambda slot, pos, count: (slot, 0, 0))
    shape = (slots, modes, size)

    def advance(scale, now, now_copy, before):
        return apply_call(
            functools.partial(step_kernel, scale),
            positions,
            own_count,
            gather_rows(now_copy, 0),
            stiffness,
            (now, before),
            [block(), block()],
            (jax.ShapeDtypeStruct(shape, jnp.float32), jax.ShapeDtypeStruct(shape, jnp.bfloat16)),
            (block(), block()),
        )

    x0 = jnp.swapaxes(start_basis.reshape(modes, slots, size), 0, 1) * live[:, None, None]
    y1, y1_copy = advance(1.0, x0, x0.astype(jnp.bfloat16), x0)
    y2, y2_copy = advance(2.0, y1, y1_copy, x0)
    y3, y3_copy = advance(2.0, y2, y2_copy, y1)

    blocks, every = gather_rows(y3_copy, 1, line=True)
    all_modes = groups * modes
    all_block = lambda: pl.BlockSpec(
        (groups, 1, modes, size), lambda slot, *unused: (0, slot, 0, 0)
    )
    sums = apply_call(
        last_kernel,
        positions,
        own_count,
        blocks,
        stiffness,
        (y3_copy, every),
        [block(), all_block()],
        jax.ShapeDtypeStruct((2 * modes, all_modes), jnp.float32),
        pl.BlockSpec((2 * modes, all_modes), lambda slot, *unused: (0, 0)),
    )
    part = modes // rows
    shares = reduce_sums(jnp.swapaxes(sums.reshape(2, rows, part, all_modes), 0, 1))
    shares = gather_rows(shares.reshape(groups * 2, part, all_modes), 2)
    shares = shares.reshape(rows, groups, 2, part, all_modes)
    gram = jnp.swapaxes(shares[:, :, 0], 0, 1).reshape(all_modes, all_modes)
    images = jnp.swapaxes(shares[:, :, 1], 0, 1).reshape(all_modes, all_modes)
    gram = gram / total + ridge_shift * jnp.eye(all_modes, dtype=jnp.float32)
    inverse = factor_inverse(gram)
    own_inverse = lax.dynamic_slice_in_dim(inverse, lax.axis_index("col") * modes, modes, 0)
    ritz = pl.pallas_call(
        ritz_kernel,
        grid=(slots,),
        in_specs=[pl.BlockSpec((modes, all_modes), lambda slot: (0, 0)), all_block()],
        out_specs=pl.BlockSpec((modes, size), lambda slot: (0, slot)),
        out_shape=jax.ShapeDtypeStruct((modes, slots * size), jnp.float32),
    )(own_inverse.astype(jnp.bfloat16), every)
    turned = dot(own_inverse, images)
    projected = dot(turned, inverse, NT) / total
    return (ritz, projected)


def solution(mesh):
    in_specs = (P("row", None, None, None), P("row", None), P(), P("col", "row"))
    out_specs = (P("col", "row"), P("col", None))
    return jax.shard_map(local, mesh=mesh, in_specs=in_specs, out_specs=out_specs, check_vma=False)
```

```python
import functools

import jax
import jax.numpy as jnp
from jax import lax
from jax.experimental import pallas as pl
from jax.experimental.pallas import tpu as pltpu
from jax.sharding import PartitionSpec as P

center_value = 4.0
half_width = 1.5
ridge_shift = 0.5

MESH = pl.DeviceIdType.MESH
HIGH = lax.Precision.HIGHEST
NT = (((1,), (1,)), ((), ()))
NN = (((1,), (0,)), ((), ()))


def line_copy(panel_ref, every_ref, sems, step, side):
    me = lax.axis_index("col")
    groups = every_ref.shape[0]
    target = me + side
    source = me - side * step
    sends = (target >= 0) & (target < groups) & (source >= 0) & (source < groups)
    origin = source - side
    receives = (origin >= 0) & (origin < groups)
    number = 2 * step + (1 if side > 0 else 0)
    bounded = lax.rem(source + groups, groups)
    return sends, receives, pltpu.make_async_remote_copy(
        src_ref=panel_ref if step == 0 else every_ref.at[bounded],
        dst_ref=every_ref.at[bounded],
        send_sem=sems.at[0, number],
        recv_sem=sems.at[1, number],
        device_id={"col": lax.rem(target + groups, groups)},
        device_id_type=MESH,
    )


def gather_kernel(slots, line, own_ref, out_ref, *refs):
    if line:
        every_ref, send_sems, recv_sems, local_sem, line_sems = refs
    else:
        send_sems, recv_sems, local_sem = refs
    me = lax.axis_index("row")
    half = slots // 2
    core = me % 2
    along_x = (me // 2) % 2
    along_y = me // 4
    mate = me + 1 - 2 * core
    beside = me + 2 - 4 * along_x
    above = me + 4 - 8 * along_y
    across = beside + 4 - 8 * along_y

    barrier = pltpu.get_barrier_semaphore()
    for other in (mate, beside, above):
        pl.semaphore_signal(barrier, inc=1, device_id={"row": other}, device_id_type=MESH)
    if line:
        groups = every_ref.shape[0]
        level = lax.axis_index("col")

        @pl.when(level > 0)
        def _():
            pl.semaphore_signal(barrier, inc=1, device_id={"col": level - 1}, device_id_type=MESH)

        @pl.when(level < groups - 1)
        def _():
            pl.semaphore_signal(barrier, inc=1, device_id={"col": level + 1}, device_id_type=MESH)

        neighbours = (level > 0).astype(jnp.int32) + (level < groups - 1).astype(jnp.int32)
        pl.semaphore_wait(barrier, 3 + neighbours)
    else:
        pl.semaphore_wait(barrier, 3)

    def line_start(step):
        for side in (-1, 1):
            sends, _, copy = line_copy(own_ref, every_ref, line_sems, step, side)
            pl.when(sends)(copy.start)

    def line_wait(step):
        for side in (-1, 1):
            _, receives, copy = line_copy(own_ref, every_ref, line_sems, step, side)
            pl.when(receives & (level - side >= 0) & (level - side < groups))(copy.wait_recv)

    def line_end(step):
        for side in (-1, 1):
            sends, _, copy = line_copy(own_ref, every_ref, line_sems, step, side)
            pl.when(sends)(copy.wait_send)

    def place(device, part):
        return out_ref.at[pl.ds(device * slots + part * half, half)]

    def own(part):
        return own_ref.at[pl.ds(part * half, half)]

    def send(number, source, device, part, target):
        return pltpu.make_async_remote_copy(
            src_ref=source,
            dst_ref=place(device, part),
            send_sem=send_sems.at[number],
            recv_sem=recv_sems.at[number],
            device_id={"row": target},
            device_id_type=MESH,
        )

    copies = [
        send(0, own(0), me, 0, beside),
        send(1, own(1), me, 1, beside),
        send(2, own(0), me, 0, above),
        send(3, own(1), me, 1, above),
        send(4, place(beside, 0), beside, 0, above),
        send(5, place(above, 1), above, 1, beside),
        send(6, own(0), me, 0, mate),
        send(7, own(1), me, 1, mate),
        send(8, place(beside, 0), beside, 0, mate),
        send(9, place(beside, 1), beside, 1, mate),
        send(10, place(above, 0), above, 0, mate),
        send(11, place(above, 1), above, 1, mate),
        send(12, place(across, 0), across, 0, mate),
        send(13, place(across, 1), across, 1, mate),
    ]
    for number in (0, 3, 1, 2, 6, 7):
        copies[number].start()
    keep = [pltpu.make_async_copy(own_ref, out_ref.at[pl.ds(me * slots, slots)], local_sem.at[0])]
    if line:
        line_start(0)
        keep.append(pltpu.make_async_copy(own_ref, every_ref.at[level], local_sem.at[1]))
    for copy in keep:
        copy.start()
    for arrived, onward in ((0, (4, 8)), (3, (5, 11)), (1, (9,)), (2, (10,))):
        copies[arrived].wait_recv()
        for number in onward:
            copies[number].start()
    if line:
        line_wait(0)
        line_start(1)
    for arrived, onward in ((4, 12), (5, 13)):
        copies[arrived].wait_recv()
        copies[onward].start()
    for number in range(6, 14):
        copies[number].wait_recv()
    if line:
        for step in range(1, groups - 1):
            line_wait(step)
            if step < groups - 2:
                line_start(step + 1)
        for step in range(groups - 1):
            line_end(step)
    for copy in keep:
        copy.wait()
    for copy in copies:
        copy.wait_send()


def gather_rows(panel, number, line=False):
    slots, modes, size = panel.shape
    rows, groups = lax.axis_size("row"), lax.axis_size("col")
    if rows != 8 or groups < 3:
        out = lax.all_gather(panel, "row", axis=0, tiled=True)
        return (out, lax.all_gather(panel, "col", axis=0, tiled=False)) if line else out
    out_shape = [jax.ShapeDtypeStruct((rows * slots, modes, size), panel.dtype)]
    scratch = [
        pltpu.SemaphoreType.DMA((14,)),
        pltpu.SemaphoreType.DMA((14,)),
        pltpu.SemaphoreType.DMA((2,)),
    ]
    if line:
        out_shape.append(jax.ShapeDtypeStruct((groups, slots, modes, size), panel.dtype))
        scratch.append(pltpu.SemaphoreType.DMA((2, 2 * (groups - 1))))
    out = pl.pallas_call(
        functools.partial(gather_kernel, slots, line),
        out_shape=out_shape,
        in_specs=[pl.BlockSpec(memory_space=pl.ANY)],
        out_specs=[pl.BlockSpec(memory_space=pl.ANY)] * len(out_shape),
        scratch_shapes=scratch,
        compiler_params=pltpu.CompilerParams(collective_id=number, has_side_effects=True),
        name="gather_both" if line else "gather_rows",
    )(panel)
    return out if line else out[0]


def reduce_kernel(sums_ref, out_ref, landed, total, row_sems, col_sems):
    rows, groups = landed.shape[0], total.shape[0]
    me, level = lax.axis_index("row"), lax.axis_index("col")
    peers = [lax.rem(me + shift, rows) for shift in range(1, rows)]
    levels = [lax.rem(level + shift, groups) for shift in range(1, groups)]
    barrier = pltpu.get_barrier_semaphore()
    for peer in peers:
        pl.semaphore_signal(barrier, inc=1, device_id={"row": peer}, device_id_type=MESH)
    for other in levels:
        pl.semaphore_signal(barrier, inc=1, device_id={"col": other}, device_id_type=MESH)
    pl.semaphore_wait(barrier, rows + groups - 2)
    shares = []
    for number, peer in enumerate(peers):
        copy = pltpu.make_async_remote_copy(
            src_ref=sums_ref.at[peer],
            dst_ref=landed.at[number],
            send_sem=row_sems.at[0, number],
            recv_sem=row_sems.at[1, number],
            device_id={"row": peer},
            device_id_type=MESH,
        )
        copy.start()
        shares.append(copy)
    share = sums_ref[me]
    for number, copy in enumerate(shares):
        copy.wait_recv()
        share = share + landed[number]
    total[0] = share
    out_ref[level] = share
    exchanges = []
    for number, other in enumerate(levels):
        copy = pltpu.make_async_remote_copy(
            src_ref=total.at[0],
            dst_ref=total.at[number + 1],
            send_sem=col_sems.at[0, number],
            recv_sem=col_sems.at[1, number],
            device_id={"col": other},
            device_id_type=MESH,
        )
        copy.start()
        exchanges.append(copy)
    for number, copy in enumerate(exchanges):
        copy.wait_recv()
        out_ref[lax.rem(level + groups - number - 1, groups)] = total[number + 1]
    for copy in shares + exchanges:
        copy.wait_send()


def reduce_sums(sums):
    rows, groups = lax.axis_size("row"), lax.axis_size("col")
    if rows != 8 or groups < 3:
        share = lax.psum_scatter(sums, "row", scatter_dimension=0, tiled=False)
        return lax.all_gather(share, "col", axis=0, tiled=False)
    return pl.pallas_call(
        reduce_kernel,
        out_shape=jax.ShapeDtypeStruct((groups, *sums.shape[1:]), sums.dtype),
        in_specs=[pl.BlockSpec(memory_space=pltpu.VMEM)],
        out_specs=pl.BlockSpec(memory_space=pltpu.VMEM),
        scratch_shapes=[
            pltpu.VMEM(sums.shape, sums.dtype),
            pltpu.VMEM((groups, *sums.shape[1:]), sums.dtype),
            pltpu.SemaphoreType.DMA((2, rows)),
            pltpu.SemaphoreType.DMA((2, groups)),
        ],
        compiler_params=pltpu.CompilerParams(collective_id=3, has_side_effects=True),
        name="reduce_sums",
    )(sums)


def product(positions, blocks_ref, stiff_ref):
    slot = pl.program_id(0)
    neighbours = stiff_ref.shape[1]
    picked = jnp.concatenate([blocks_ref[positions[slot, k]] for k in range(neighbours)], axis=1)
    stored = jnp.concatenate([stiff_ref[0, k] for k in range(neighbours)], axis=1)
    return lax.dot_general(picked, stored, NT, preferred_element_type=jnp.float32)


def step_kernel(scale, positions, own_count, blocks_ref, stiff_ref, now_ref, before_ref, out_ref, copy_ref):
    live = pl.program_id(0) < own_count[0]

    @pl.when(live)
    def _():
        now = now_ref[0]
        result = (product(positions, blocks_ref, stiff_ref) - center_value * now) * (scale / half_width)
        if scale == 2.0:
            result = result - before_ref[0]
        out_ref[0] = result
        copy_ref[0] = result.astype(copy_ref.dtype)

    @pl.when(jnp.logical_not(live))
    def _():
        out_ref[...] = jnp.zeros_like(out_ref)
        copy_ref[...] = jnp.zeros_like(copy_ref)


def last_kernel(positions, own_count, blocks_ref, stiff_ref, now_ref, all_ref, out_ref):
    slot = pl.program_id(0)

    @pl.when(slot == 0)
    def _():
        out_ref[...] = jnp.zeros_like(out_ref)

    @pl.when(slot < own_count[0])
    def _():
        image = product(positions, blocks_ref, stiff_ref).astype(jnp.bfloat16)
        left = jnp.concatenate([now_ref[0], image], axis=0)
        whole = all_ref[...].reshape(-1, all_ref.shape[-1])
        out_ref[...] += lax.dot_general(left, whole, NT, preferred_element_type=jnp.float32)


def apply_call(kernel, positions, own_count, blocks, stiffness, extra, extra_specs, out_shape, out_specs):
    slots, neighbours, size, _ = stiffness.shape
    last = lambda slot, pos, count: (jnp.minimum(slot, count[0] - 1), 0, 0, 0)
    return pl.pallas_call(
        kernel,
        grid_spec=pltpu.PrefetchScalarGridSpec(
            num_scalar_prefetch=2,
            grid=(slots,),
            in_specs=[
                pl.BlockSpec(memory_space=pltpu.VMEM),
                pl.BlockSpec((1, neighbours, size, size), last),
                *extra_specs,
            ],
            out_specs=out_specs,
        ),
        out_shape=out_shape,
        compiler_params=pltpu.CompilerParams(vmem_limit_bytes=40 * 2**20),
    )(positions, own_count, blocks, stiffness, *extra)


def eliminate(block_ref, work_ref):
    size = block_ref.shape[0]
    rows = lax.broadcasted_iota(jnp.int32, (size, size), 0)
    columns = lax.broadcasted_iota(jnp.int32, (size, size), 1)
    work_ref[...] = (rows == columns).astype(jnp.float32)
    down = lax.broadcasted_iota(jnp.int32, (size, 1), 0)
    across = lax.broadcasted_iota(jnp.int32, (1, size), 1)

    def step(k, carry):
        pivot_row = block_ref[pl.ds(k, 1), :]
        work_row = work_ref[pl.ds(k, 1), :]
        pivot = jnp.sum(jnp.where(across == k, pivot_row, 0.0), axis=1, keepdims=True)
        root = lax.rsqrt(pivot)
        block = block_ref[...]
        column = jnp.sum(jnp.where(columns == k, block, 0.0), axis=1, keepdims=True)
        factor = jnp.where(down > k, column * (root * root), 0.0)
        block_ref[...] = block - factor * pivot_row
        work_ref[...] = jnp.where(down == k, work_ref[...] * root, work_ref[...] - factor * work_row)
        return carry

    lax.fori_loop(0, size, step, 0)


def dot(a, b, dims=NN):
    return lax.dot_general(a, b, dims, precision=HIGH, preferred_element_type=jnp.float32)


def exact_factor(gram_ref, inverse_ref, trail, block_ref, work_ref):
    modes = gram_ref.shape[0]
    size = block_ref.shape[0]
    trail[...] = gram_ref[...]
    inverse_ref[...] = jnp.zeros_like(inverse_ref)
    for start in range(0, modes, size):
        end = start + size
        block_ref[...] = trail[start:end, start:end]
        eliminate(block_ref, work_ref)
        own = work_ref[...]
        inverse_ref[start:end, start:end] = own
        if start:
            left = dot(trail[start:end, :start], inverse_ref[:start, :start])
            inverse_ref[start:end, :start] = -dot(own, left)
        if end < modes:
            panel = dot(trail[end:, start:end], own, NT)
            trail[end:, start:end] = panel
            trail[end:, end:] = trail[end:, end:] - dot(panel, panel, NT)


def split(a):
    high = a.astype(jnp.bfloat16)
    return high, (a - high.astype(jnp.float32)).astype(jnp.bfloat16)


def one_pass(a, b, dims=NN):
    return lax.dot_general(
        a.astype(jnp.bfloat16), b.astype(jnp.bfloat16), dims, preferred_element_type=jnp.float32
    )


def three_pass(a, b, dims=NN):
    (a_high, a_low), (b_high, b_low) = split(a), split(b)
    go = lambda x, y: lax.dot_general(x, y, dims, preferred_element_type=jnp.float32)
    return go(a_high, b_high) + (go(a_high, b_low) + go(a_low, b_high))


def factor_kernel(gram_ref, inverse_ref, trail, block_ref, work_ref):
    modes = gram_ref.shape[0]
    down = lax.broadcasted_iota(jnp.int32, (modes, modes), 0)
    across = lax.broadcasted_iota(jnp.int32, (modes, modes), 1)
    diagonal = jnp.where(down == across, 1.0, 0.0)
    weight = jnp.where(down > across, 1.0, 0.5 * diagonal)
    trail[...] = gram_ref[...]
    variance = jnp.sum(trail[...] * diagonal, axis=1, keepdims=True)
    inverse_ref[...] = diagonal * lax.rsqrt(variance)

    def refine(multiply, limit, most):
        def going(state):
            return (state[0] < most) & (state[1] > limit)

        def step(state):
            now = inverse_ref[...]
            error = multiply(multiply(now, trail[...]), now, NT) - diagonal
            inverse_ref[...] = now - multiply(error * weight, now)
            return state[0] + 1, jnp.max(jnp.abs(error))

        return lax.while_loop(going, step, (jnp.int32(0), jnp.float32(1e30)))[1]

    refine(one_pass, 0.06, 12)
    error = refine(three_pass, 5e-4, 6)
    least = jnp.min(jnp.where(down == across, inverse_ref[...], 1.0))
    good = (error <= 5e-4) & (least > 0.0)

    @pl.when(jnp.logical_not(good))
    def _():
        exact_factor(gram_ref, inverse_ref, trail, block_ref, work_ref)


def factor_inverse(gram):
    modes = gram.shape[0]
    return pl.pallas_call(
        factor_kernel,
        out_shape=jax.ShapeDtypeStruct((modes, modes), jnp.float32),
        in_specs=[pl.BlockSpec(memory_space=pltpu.VMEM)],
        out_specs=pl.BlockSpec(memory_space=pltpu.VMEM),
        scratch_shapes=[
            pltpu.VMEM((modes, modes), jnp.float32),
            pltpu.VMEM((128, 128), jnp.float32),
            pltpu.VMEM((128, 128), jnp.float32),
        ],
        compiler_params=pltpu.CompilerParams(vmem_limit_bytes=32 * 2**20),
        name="factor_inverse",
    )(gram)


def ritz_kernel(rows_ref, all_ref, out_ref):
    groups, slots, modes, size = all_ref.shape
    rows = rows_ref[...]
    for slot in range(slots):
        whole = all_ref[:, slot].reshape(groups * modes, size)
        out_ref[:, slot * size : (slot + 1) * size] = lax.dot_general(
            rows, whole, NN, preferred_element_type=jnp.float32
        )


def local(stiffness, block_cols, block_row_counts, start_basis):
    slots, neighbours, size, _ = stiffness.shape
    modes = start_basis.shape[0]
    groups = lax.axis_size("col")
    rows = block_row_counts.shape[0]
    row_position = lax.axis_index("row")
    ids = jnp.arange(rows, dtype=jnp.int32)
    starts = jnp.sum(jnp.where(ids[None, :] < ids[:, None], block_row_counts[None, :], 0), 1)
    ends = starts + block_row_counts
    own_count = jnp.sum(jnp.where(ids == row_position, block_row_counts, 0))
    passed = (ends[None, None, :] <= block_cols[:, :, None]).astype(jnp.int32)
    owner = jnp.sum(passed, 2)
    first = jnp.sum(passed * block_row_counts[None, None, :], 2)
    positions = (owner * slots + block_cols - first).astype(jnp.int32)
    total = (jnp.sum(block_row_counts) * size).astype(jnp.float32)
    live = (jnp.arange(slots) < own_count).astype(jnp.float32)
    own_count = own_count.reshape(1)

    block = lambda: pl.BlockSpec((1, modes, size), lambda slot, pos, count: (slot, 0, 0))
    shape = (slots, modes, size)

    def advance(scale, now, now_copy, before):
        return apply_call(
            functools.partial(step_kernel, scale),
            positions,
            own_count,
            gather_rows(now_copy, 0),
            stiffness,
            (now, before),
            [block(), block()],
            (jax.ShapeDtypeStruct(shape, jnp.float32), jax.ShapeDtypeStruct(shape, jnp.bfloat16)),
            (block(), block()),
        )

    x0 = jnp.swapaxes(start_basis.reshape(modes, slots, size), 0, 1) * live[:, None, None]
    y1, y1_copy = advance(1.0, x0, x0.astype(jnp.bfloat16), x0)
    y2, y2_copy = advance(2.0, y1, y1_copy, x0)
    y3, y3_copy = advance(2.0, y2, y2_copy, y1)

    blocks, every = gather_rows(y3_copy, 1, line=True)
    all_modes = groups * modes
    all_block = lambda: pl.BlockSpec(
        (groups, 1, modes, size), lambda slot, *unused: (0, slot, 0, 0)
    )
    sums = apply_call(
        last_kernel,
        positions,
        own_count,
        blocks,
        stiffness,
        (y3_copy, every),
        [block(), all_block()],
        jax.ShapeDtypeStruct((2 * modes, all_modes), jnp.float32),
        pl.BlockSpec((2 * modes, all_modes), lambda slot, *unused: (0, 0)),
    )
    part = modes // rows
    shares = reduce_sums(jnp.swapaxes(sums.reshape(2, rows, part, all_modes), 0, 1))
    shares = gather_rows(shares.reshape(groups * 2, part, all_modes), 2)
    shares = shares.reshape(rows, groups, 2, part, all_modes)
    gram = jnp.swapaxes(shares[:, :, 0], 0, 1).reshape(all_modes, all_modes)
    images = jnp.swapaxes(shares[:, :, 1], 0, 1).reshape(all_modes, all_modes)
    gram = gram / total + ridge_shift * jnp.eye(all_modes, dtype=jnp.float32)
    inverse = factor_inverse(gram)
    own_inverse = lax.dynamic_slice_in_dim(inverse, lax.axis_index("col") * modes, modes, 0)
    width = 4 if slots % 4 == 0 else 1
    ritz = pl.pallas_call(
        ritz_kernel,
        grid=(slots // width,),
        in_specs=[
            pl.BlockSpec((modes, all_modes), lambda step: (0, 0)),
            pl.BlockSpec((groups, width, modes, size), lambda step: (0, step, 0, 0)),
        ],
        out_specs=pl.BlockSpec((modes, width * size), lambda step: (0, step)),
        out_shape=jax.ShapeDtypeStruct((modes, slots * size), jnp.float32),
    )(own_inverse.astype(jnp.bfloat16), every)
    turned = dot(own_inverse, images)
    projected = dot(turned, inverse, NT) / total
    return (ritz, projected)


def solution(mesh):
    in_specs = (P("row", None, None, None), P("row", None), P(), P("col", "row"))
    out_specs = (P("col", "row"), P("col", None))
    return jax.shard_map(local, mesh=mesh, in_specs=in_specs, out_specs=out_specs, check_vma=False)
```

```python
import functools

import jax
import jax.numpy as jnp
from jax import lax
from jax.experimental import pallas as pl
from jax.experimental.pallas import tpu as pltpu
from jax.sharding import PartitionSpec as P

center_value = 4.0
half_width = 1.5
ridge_shift = 0.5

MESH = pl.DeviceIdType.MESH
HIGH = lax.Precision.HIGHEST
NT = (((1,), (1,)), ((), ()))
NN = (((1,), (0,)), ((), ()))


def line_copy(panel_ref, every_ref, sems, step, side):
    me = lax.axis_index("col")
    groups = every_ref.shape[0]
    target = me + side
    source = me - side * step
    sends = (target >= 0) & (target < groups) & (source >= 0) & (source < groups)
    origin = source - side
    receives = (origin >= 0) & (origin < groups)
    number = 2 * step + (1 if side > 0 else 0)
    bounded = lax.rem(source + groups, groups)
    return sends, receives, pltpu.make_async_remote_copy(
        src_ref=panel_ref if step == 0 else every_ref.at[bounded],
        dst_ref=every_ref.at[bounded],
        send_sem=sems.at[0, number],
        recv_sem=sems.at[1, number],
        device_id={"col": lax.rem(target + groups, groups)},
        device_id_type=MESH,
    )


def gather_kernel(slots, line, own_ref, out_ref, *refs):
    if line:
        every_ref, send_sems, recv_sems, local_sem, line_sems = refs
    else:
        send_sems, recv_sems, local_sem = refs
    me = lax.axis_index("row")
    half = slots // 2
    core = me % 2
    along_x = (me // 2) % 2
    along_y = me // 4
    mate = me + 1 - 2 * core
    beside = me + 2 - 4 * along_x
    above = me + 4 - 8 * along_y
    across = beside + 4 - 8 * along_y

    barrier = pltpu.get_barrier_semaphore()
    for other in (mate, beside, above):
        pl.semaphore_signal(barrier, inc=1, device_id={"row": other}, device_id_type=MESH)
    if line:
        groups = every_ref.shape[0]
        level = lax.axis_index("col")

        @pl.when(level > 0)
        def _():
            pl.semaphore_signal(barrier, inc=1, device_id={"col": level - 1}, device_id_type=MESH)

        @pl.when(level < groups - 1)
        def _():
            pl.semaphore_signal(barrier, inc=1, device_id={"col": level + 1}, device_id_type=MESH)

        neighbours = (level > 0).astype(jnp.int32) + (level < groups - 1).astype(jnp.int32)
        pl.semaphore_wait(barrier, 3 + neighbours)
    else:
        pl.semaphore_wait(barrier, 3)

    def line_start(step):
        for side in (-1, 1):
            sends, _, copy = line_copy(own_ref, every_ref, line_sems, step, side)
            pl.when(sends)(copy.start)

    def line_wait(step):
        for side in (-1, 1):
            _, receives, copy = line_copy(own_ref, every_ref, line_sems, step, side)
            pl.when(receives & (level - side >= 0) & (level - side < groups))(copy.wait_recv)

    def line_end(step):
        for side in (-1, 1):
            sends, _, copy = line_copy(own_ref, every_ref, line_sems, step, side)
            pl.when(sends)(copy.wait_send)

    def place(device, part):
        return out_ref.at[pl.ds(device * slots + part * half, half)]

    def own(part):
        return own_ref.at[pl.ds(part * half, half)]

    def send(number, source, device, part, target):
        return pltpu.make_async_remote_copy(
            src_ref=source,
            dst_ref=place(device, part),
            send_sem=send_sems.at[number],
            recv_sem=recv_sems.at[number],
            device_id={"row": target},
            device_id_type=MESH,
        )

    copies = [
        send(0, own(0), me, 0, beside),
        send(1, own(1), me, 1, beside),
        send(2, own(0), me, 0, above),
        send(3, own(1), me, 1, above),
        send(4, place(beside, 0), beside, 0, above),
        send(5, place(above, 1), above, 1, beside),
        send(6, own(0), me, 0, mate),
        send(7, own(1), me, 1, mate),
        send(8, place(beside, 0), beside, 0, mate),
        send(9, place(beside, 1), beside, 1, mate),
        send(10, place(above, 0), above, 0, mate),
        send(11, place(above, 1), above, 1, mate),
        send(12, place(across, 0), across, 0, mate),
        send(13, place(across, 1), across, 1, mate),
    ]
    for number in (0, 3, 1, 2, 6, 7):
        copies[number].start()
    keep = [pltpu.make_async_copy(own_ref, out_ref.at[pl.ds(me * slots, slots)], local_sem.at[0])]
    if line:
        line_start(0)
        keep.append(pltpu.make_async_copy(own_ref, every_ref.at[level], local_sem.at[1]))
    for copy in keep:
        copy.start()
    for arrived, onward in ((0, (4, 8)), (3, (5, 11)), (1, (9,)), (2, (10,))):
        copies[arrived].wait_recv()
        for number in onward:
            copies[number].start()
    if line:
        line_wait(0)
        line_start(1)
    for arrived, onward in ((4, 12), (5, 13)):
        copies[arrived].wait_recv()
        copies[onward].start()
    for number in range(6, 14):
        copies[number].wait_recv()
    if line:
        for step in range(1, groups - 1):
            line_wait(step)
            if step < groups - 2:
                line_start(step + 1)
        for step in range(groups - 1):
            line_end(step)
    for copy in keep:
        copy.wait()
    for copy in copies:
        copy.wait_send()


def gather_rows(panel, number, line=False):
    slots, modes, size = panel.shape
    rows, groups = lax.axis_size("row"), lax.axis_size("col")
    if rows != 8 or groups < 3:
        out = lax.all_gather(panel, "row", axis=0, tiled=True)
        return (out, lax.all_gather(panel, "col", axis=0, tiled=False)) if line else out
    out_shape = [jax.ShapeDtypeStruct((rows * slots, modes, size), panel.dtype)]
    scratch = [
        pltpu.SemaphoreType.DMA((14,)),
        pltpu.SemaphoreType.DMA((14,)),
        pltpu.SemaphoreType.DMA((2,)),
    ]
    if line:
        out_shape.append(jax.ShapeDtypeStruct((groups, slots, modes, size), panel.dtype))
        scratch.append(pltpu.SemaphoreType.DMA((2, 2 * (groups - 1))))
    out = pl.pallas_call(
        functools.partial(gather_kernel, slots, line),
        out_shape=out_shape,
        in_specs=[pl.BlockSpec(memory_space=pl.ANY)],
        out_specs=[pl.BlockSpec(memory_space=pl.ANY)] * len(out_shape),
        scratch_shapes=scratch,
        compiler_params=pltpu.CompilerParams(collective_id=number, has_side_effects=True),
        name="gather_both" if line else "gather_rows",
    )(panel)
    return out if line else out[0]


def reduce_kernel(sums_ref, out_ref, landed, total, row_sems, col_sems):
    rows, groups = landed.shape[0], total.shape[0]
    me, level = lax.axis_index("row"), lax.axis_index("col")
    peers = [lax.rem(me + shift, rows) for shift in range(1, rows)]
    levels = [lax.rem(level + shift, groups) for shift in range(1, groups)]
    barrier = pltpu.get_barrier_semaphore()
    for peer in peers:
        pl.semaphore_signal(barrier, inc=1, device_id={"row": peer}, device_id_type=MESH)
    for other in levels:
        pl.semaphore_signal(barrier, inc=1, device_id={"col": other}, device_id_type=MESH)
    pl.semaphore_wait(barrier, rows + groups - 2)
    shares = []
    for number, peer in enumerate(peers):
        copy = pltpu.make_async_remote_copy(
            src_ref=sums_ref.at[peer],
            dst_ref=landed.at[number],
            send_sem=row_sems.at[0, number],
            recv_sem=row_sems.at[1, number],
            device_id={"row": peer},
            device_id_type=MESH,
        )
        copy.start()
        shares.append(copy)
    share = sums_ref[me]
    for number, copy in enumerate(shares):
        copy.wait_recv()
        share = share + landed[number]
    total[0] = share
    out_ref[level] = share
    exchanges = []
    for number, other in enumerate(levels):
        copy = pltpu.make_async_remote_copy(
            src_ref=total.at[0],
            dst_ref=total.at[number + 1],
            send_sem=col_sems.at[0, number],
            recv_sem=col_sems.at[1, number],
            device_id={"col": other},
            device_id_type=MESH,
        )
        copy.start()
        exchanges.append(copy)
    for number, copy in enumerate(exchanges):
        copy.wait_recv()
        out_ref[lax.rem(level + groups - number - 1, groups)] = total[number + 1]
    for copy in shares + exchanges:
        copy.wait_send()


def reduce_sums(sums):
    rows, groups = lax.axis_size("row"), lax.axis_size("col")
    if rows != 8 or groups < 3:
        share = lax.psum_scatter(sums, "row", scatter_dimension=0, tiled=False)
        return lax.all_gather(share, "col", axis=0, tiled=False)
    return pl.pallas_call(
        reduce_kernel,
        out_shape=jax.ShapeDtypeStruct((groups, *sums.shape[1:]), sums.dtype),
        in_specs=[pl.BlockSpec(memory_space=pltpu.VMEM)],
        out_specs=pl.BlockSpec(memory_space=pltpu.VMEM),
        scratch_shapes=[
            pltpu.VMEM(sums.shape, sums.dtype),
            pltpu.VMEM((groups, *sums.shape[1:]), sums.dtype),
            pltpu.SemaphoreType.DMA((2, rows)),
            pltpu.SemaphoreType.DMA((2, groups)),
        ],
        compiler_params=pltpu.CompilerParams(collective_id=3, has_side_effects=True),
        name="reduce_sums",
    )(sums)


def product(positions, slot, blocks_ref, stored_ref):
    neighbours = stored_ref.shape[0]
    picked = jnp.concatenate([blocks_ref[positions[slot, k]] for k in range(neighbours)], axis=1)
    stored = jnp.concatenate([stored_ref[k] for k in range(neighbours)], axis=1)
    return lax.dot_general(picked, stored, NT, preferred_element_type=jnp.float32)


def step_kernel(scale, positions, own_count, blocks_ref, stiff_ref, now_ref, before_ref, out_ref, copy_ref):
    width = stiff_ref.shape[0]

    def one(i, slot):
        @pl.when(slot < own_count[0])
        def _():
            now = now_ref[i]
            result = product(positions, slot, blocks_ref, stiff_ref.at[i]) - center_value * now
            result = result * (scale / half_width)
            if scale == 2.0:
                result = result - before_ref[i]
            out_ref[i] = result
            copy_ref[i] = result.astype(copy_ref.dtype)

        @pl.when(slot >= own_count[0])
        def _():
            out_ref[i] = jnp.zeros(out_ref.shape[1:], out_ref.dtype)
            copy_ref[i] = jnp.zeros(copy_ref.shape[1:], copy_ref.dtype)

    for i in range(width):
        one(i, pl.program_id(0) * width + i)


def last_kernel(positions, own_count, blocks_ref, stiff_ref, now_ref, all_ref, out_ref, left_ref):
    groups, width, modes, size = all_ref.shape
    first = pl.program_id(0) * width

    @pl.when(first == 0)
    def _():
        out_ref[...] = jnp.zeros_like(out_ref)

    def one(i, slot):
        left_ref[:modes, i * size : (i + 1) * size] = now_ref[i]

        @pl.when(slot < own_count[0])
        def _():
            image = product(positions, slot, blocks_ref, stiff_ref.at[i])
            left_ref[modes:, i * size : (i + 1) * size] = image.astype(left_ref.dtype)

        @pl.when(slot >= own_count[0])
        def _():
            left_ref[modes:, i * size : (i + 1) * size] = jnp.zeros((modes, size), left_ref.dtype)

    @pl.when(first < own_count[0])
    def _():
        for i in range(width):
            one(i, first + i)
        whole = jnp.concatenate(
            [all_ref[:, i].reshape(groups * modes, size) for i in range(width)], axis=1
        )
        out_ref[...] += lax.dot_general(left_ref[...], whole, NT, preferred_element_type=jnp.float32)


def apply_call(
    kernel, width, positions, own_count, blocks, stiffness, extra, extra_specs, out_shape, out_specs, scratch=()
):
    slots, neighbours, size, _ = stiffness.shape
    last = lambda step, pos, count: (jnp.minimum(step, lax.div(count[0] - 1, width)), 0, 0, 0)
    return pl.pallas_call(
        kernel,
        grid_spec=pltpu.PrefetchScalarGridSpec(
            num_scalar_prefetch=2,
            grid=(slots // width,),
            in_specs=[
                pl.BlockSpec(memory_space=pltpu.VMEM),
                pl.BlockSpec((width, neighbours, size, size), last),
                *extra_specs,
            ],
            out_specs=out_specs,
            scratch_shapes=list(scratch),
        ),
        out_shape=out_shape,
        compiler_params=pltpu.CompilerParams(vmem_limit_bytes=40 * 2**20),
    )(positions, own_count, blocks, stiffness, *extra)


def eliminate(block_ref, work_ref):
    size = block_ref.shape[0]
    rows = lax.broadcasted_iota(jnp.int32, (size, size), 0)
    columns = lax.broadcasted_iota(jnp.int32, (size, size), 1)
    work_ref[...] = (rows == columns).astype(jnp.float32)
    down = lax.broadcasted_iota(jnp.int32, (size, 1), 0)
    across = lax.broadcasted_iota(jnp.int32, (1, size), 1)

    def step(k, carry):
        pivot_row = block_ref[pl.ds(k, 1), :]
        work_row = work_ref[pl.ds(k, 1), :]
        pivot = jnp.sum(jnp.where(across == k, pivot_row, 0.0), axis=1, keepdims=True)
        root = lax.rsqrt(pivot)
        block = block_ref[...]
        column = jnp.sum(jnp.where(columns == k, block, 0.0), axis=1, keepdims=True)
        factor = jnp.where(down > k, column * (root * root), 0.0)
        block_ref[...] = block - factor * pivot_row
        work_ref[...] = jnp.where(down == k, work_ref[...] * root, work_ref[...] - factor * work_row)
        return carry

    lax.fori_loop(0, size, step, 0)


def dot(a, b, dims=NN):
    return lax.dot_general(a, b, dims, precision=HIGH, preferred_element_type=jnp.float32)


def exact_factor(gram_ref, inverse_ref, trail, block_ref, work_ref):
    modes = gram_ref.shape[0]
    size = block_ref.shape[0]
    trail[...] = gram_ref[...]
    inverse_ref[...] = jnp.zeros_like(inverse_ref)
    for start in range(0, modes, size):
        end = start + size
        block_ref[...] = trail[start:end, start:end]
        eliminate(block_ref, work_ref)
        own = work_ref[...]
        inverse_ref[start:end, start:end] = own
        if start:
            left = dot(trail[start:end, :start], inverse_ref[:start, :start])
            inverse_ref[start:end, :start] = -dot(own, left)
        if end < modes:
            panel = dot(trail[end:, start:end], own, NT)
            trail[end:, start:end] = panel
            trail[end:, end:] = trail[end:, end:] - dot(panel, panel, NT)


def split(a):
    high = a.astype(jnp.bfloat16)
    return high, (a - high.astype(jnp.float32)).astype(jnp.bfloat16)


def one_pass(a, b, dims=NN):
    return lax.dot_general(
        a.astype(jnp.bfloat16), b.astype(jnp.bfloat16), dims, preferred_element_type=jnp.float32
    )


def three_pass(a, b, dims=NN):
    (a_high, a_low), (b_high, b_low) = split(a), split(b)
    go = lambda x, y: lax.dot_general(x, y, dims, preferred_element_type=jnp.float32)
    return go(a_high, b_high) + (go(a_high, b_low) + go(a_low, b_high))


def factor_kernel(gram_ref, inverse_ref, trail, block_ref, work_ref):
    modes = gram_ref.shape[0]
    down = lax.broadcasted_iota(jnp.int32, (modes, modes), 0)
    across = lax.broadcasted_iota(jnp.int32, (modes, modes), 1)
    diagonal = jnp.where(down == across, 1.0, 0.0)
    weight = jnp.where(down > across, 1.0, 0.5 * diagonal)
    trail[...] = gram_ref[...]
    variance = jnp.sum(trail[...] * diagonal, axis=1, keepdims=True)
    inverse_ref[...] = diagonal * lax.rsqrt(variance)

    def refine(multiply, limit, most):
        def going(state):
            return (state[0] < most) & (state[1] > limit)

        def step(state):
            now = inverse_ref[...]
            error = multiply(multiply(now, trail[...]), now, NT) - diagonal
            inverse_ref[...] = now - multiply(error * weight, now)
            return state[0] + 1, jnp.max(jnp.abs(error))

        return lax.while_loop(going, step, (jnp.int32(0), jnp.float32(1e30)))[1]

    refine(one_pass, 0.06, 12)
    error = refine(three_pass, 5e-4, 6)
    least = jnp.min(jnp.where(down == across, inverse_ref[...], 1.0))
    good = (error <= 5e-4) & (least > 0.0)

    @pl.when(jnp.logical_not(good))
    def _():
        exact_factor(gram_ref, inverse_ref, trail, block_ref, work_ref)


def factor_inverse(gram):
    modes = gram.shape[0]
    return pl.pallas_call(
        factor_kernel,
        out_shape=jax.ShapeDtypeStruct((modes, modes), jnp.float32),
        in_specs=[pl.BlockSpec(memory_space=pltpu.VMEM)],
        out_specs=pl.BlockSpec(memory_space=pltpu.VMEM),
        scratch_shapes=[
            pltpu.VMEM((modes, modes), jnp.float32),
            pltpu.VMEM((128, 128), jnp.float32),
            pltpu.VMEM((128, 128), jnp.float32),
        ],
        compiler_params=pltpu.CompilerParams(vmem_limit_bytes=32 * 2**20),
        name="factor_inverse",
    )(gram)


def ritz_kernel(rows_ref, all_ref, out_ref):
    groups, slots, modes, size = all_ref.shape
    rows = rows_ref[...]
    for slot in range(slots):
        whole = all_ref[:, slot].reshape(groups * modes, size)
        out_ref[:, slot * size : (slot + 1) * size] = lax.dot_general(
            rows, whole, NN, preferred_element_type=jnp.float32
        )


def local(stiffness, block_cols, block_row_counts, start_basis):
    slots, neighbours, size, _ = stiffness.shape
    modes = start_basis.shape[0]
    groups = lax.axis_size("col")
    rows = block_row_counts.shape[0]
    row_position = lax.axis_index("row")
    ids = jnp.arange(rows, dtype=jnp.int32)
    starts = jnp.sum(jnp.where(ids[None, :] < ids[:, None], block_row_counts[None, :], 0), 1)
    ends = starts + block_row_counts
    own_count = jnp.sum(jnp.where(ids == row_position, block_row_counts, 0))
    passed = (ends[None, None, :] <= block_cols[:, :, None]).astype(jnp.int32)
    owner = jnp.sum(passed, 2)
    first = jnp.sum(passed * block_row_counts[None, None, :], 2)
    positions = (owner * slots + block_cols - first).astype(jnp.int32)
    total = (jnp.sum(block_row_counts) * size).astype(jnp.float32)
    live = (jnp.arange(slots) < own_count).astype(jnp.float32)
    own_count = own_count.reshape(1)

    width = 4 if slots % 4 == 0 else 1
    block = lambda: pl.BlockSpec((width, modes, size), lambda slot, pos, count: (slot, 0, 0))
    shape = (slots, modes, size)

    def advance(scale, now, now_copy, before):
        return apply_call(
            functools.partial(step_kernel, scale),
            width,
            positions,
            own_count,
            gather_rows(now_copy, 0),
            stiffness,
            (now, before),
            [block(), block()],
            (jax.ShapeDtypeStruct(shape, jnp.float32), jax.ShapeDtypeStruct(shape, jnp.bfloat16)),
            (block(), block()),
        )

    x0 = jnp.swapaxes(start_basis.reshape(modes, slots, size), 0, 1) * live[:, None, None]
    y1, y1_copy = advance(1.0, x0, x0.astype(jnp.bfloat16), x0)
    y2, y2_copy = advance(2.0, y1, y1_copy, x0)
    y3, y3_copy = advance(2.0, y2, y2_copy, y1)

    blocks, every = gather_rows(y3_copy, 1, line=True)
    all_modes = groups * modes
    all_block = lambda: pl.BlockSpec(
        (groups, width, modes, size), lambda slot, *unused: (0, slot, 0, 0)
    )
    sums = apply_call(
        last_kernel,
        width,
        positions,
        own_count,
        blocks,
        stiffness,
        (y3_copy, every),
        [block(), all_block()],
        jax.ShapeDtypeStruct((2 * modes, all_modes), jnp.float32),
        pl.BlockSpec((2 * modes, all_modes), lambda slot, *unused: (0, 0)),
        (pltpu.VMEM((2 * modes, width * size), jnp.bfloat16),),
    )
    part = modes // rows
    shares = reduce_sums(jnp.swapaxes(sums.reshape(2, rows, part, all_modes), 0, 1))
    shares = gather_rows(shares.reshape(groups * 2, part, all_modes), 2)
    shares = shares.reshape(rows, groups, 2, part, all_modes)
    gram = jnp.swapaxes(shares[:, :, 0], 0, 1).reshape(all_modes, all_modes)
    images = jnp.swapaxes(shares[:, :, 1], 0, 1).reshape(all_modes, all_modes)
    gram = gram / total + ridge_shift * jnp.eye(all_modes, dtype=jnp.float32)
    inverse = factor_inverse(gram)
    own_inverse = lax.dynamic_slice_in_dim(inverse, lax.axis_index("col") * modes, modes, 0)
    ritz = pl.pallas_call(
        ritz_kernel,
        grid=(slots // width,),
        in_specs=[
            pl.BlockSpec((modes, all_modes), lambda step: (0, 0)),
            pl.BlockSpec((groups, width, modes, size), lambda step: (0, step, 0, 0)),
        ],
        out_specs=pl.BlockSpec((modes, width * size), lambda step: (0, step)),
        out_shape=jax.ShapeDtypeStruct((modes, slots * size), jnp.float32),
    )(own_inverse.astype(jnp.bfloat16), every)
    turned = dot(own_inverse, images)
    projected = dot(turned, inverse, NT) / total
    return (ritz, projected)


def solution(mesh):
    in_specs = (P("row", None, None, None), P("row", None), P(), P("col", "row"))
    out_specs = (P("col", "row"), P("col", None))
    return jax.shard_map(local, mesh=mesh, in_specs=in_specs, out_specs=out_specs, check_vma=False)
```
